32 devices in a mesh: clips: 2 (over y), rows: 8 (over z, x), kern: 2 (over core).
Axes of the slice: x: 2, y: 2, z: 4, core: 2. Of those that a mesh axis runs over, the one named last changes fastest.
Arguments:
- features: bfloat16 [16, 512, 256], P('kern', ('clips', 'rows')), parts along dimension 1, may hold values from -6 to 6
- head_weight: float32 [16], P('kern'), may hold values from -1.5 to 1.5
- kernels: float32 [8, 2, 128, 128], P('kern')
- kernel_weights: float32 [8], P('kern'), may hold values from 0.25 to 2
- target: bfloat16 [512, 256], P(('clips', 'rows')), parts along dimension 0, may hold values from 0 to 1
Outputs:
- grad_features: bfloat16 [16, 512, 256], P('kern', ('clips', 'rows')), parts along dimension 1
The draws below stay inside these ranges and needn't reach their ends.
There are 2 independent parts, one for each index of `clips`. The reference program is written for one: setup_inputs(seed, part) draws one part's arguments, and reference() takes and returns one part's arrays. A program takes and returns all parts, laid end to end along the dimension named above; an argument that names none is the same for every part. Nothing has to cross between parts.
All inputs are finite; a program needn't handle non-finite values.
Results may differ from the reference program's by a relative error of at most 0.001.
Values sent between devices are 32-bit elements; how exact they have to be, the bound alone decides.
A program may use at most 64 MiB of HBM per device.

```python
import math
import jax
import jax.numpy as jnp
from jax import lax

N = 256
S = 128
KERNELS = 8
CHANNELS = 16


def draw_kernels(key, part):
    frequency = (jnp.arange(S) - S // 2).astype(jnp.float32)
    radius = jnp.sqrt(frequency[:, None] * frequency[:, None] + frequency[None, :] * frequency[None, :])
    ramp = jnp.minimum(1.0, radius / (S / 4.0))
    values = jax.random.normal(key, (KERNELS, 2, S, S), jnp.float32)
    return (3.0 * values * ramp).astype(jnp.float32)


def draw_target(key, part):
    coins = jax.random.uniform(key, (N, N), jnp.float32)
    return jnp.where(coins < 0.5, 1.0, 0.0).astype(jnp.bfloat16)


def levels(rng, shape, shards, low, top_value):
    def one(dim, shards_of):
        heights = jax.random.uniform(jax.random.fold_in(jax.random.fold_in(rng, 6), dim), (shards_of,), jnp.float32, low / len(shards), top_value / len(shards))
        return jnp.repeat(jnp.exp(heights), shape[dim] // shards_of).reshape((-1,) + (1,) * (len(shape) - dim - 1))

    factor_of = one(*shards[0])
    for cut in shards[1:]:
        factor_of = factor_of * one(*cut)
    return factor_of


def scatter_about(rng, shape, width, bound, cuts=(), kind=jnp.bfloat16):
    entries = jax.random.normal(rng, shape, jnp.float32) * width
    if len(cuts) > 0:
        entries = levels(rng, shape, cuts, -0.22, 0.18) * entries
    return jnp.clip(entries, min=-bound, max=bound).astype(kind)


def setup_inputs(seed: int = 0, part: int = 0) -> dict:
    splits = jax.random.split(jax.random.key(seed), 6)
    part_keys = jax.random.split(jax.random.fold_in(splits[5], part), 6)
    features = scatter_about(part_keys[0], (CHANNELS, N, N), 1.0, 6.0, ((0, 2), (1, 8)))
    head_weight = scatter_about(splits[1], (CHANNELS,), CHANNELS ** -0.5, 1.5, ((0, 2),), jnp.float32)
    kernels = draw_kernels(jax.random.fold_in(splits[5], 71), part)
    kernel_weights = jnp.clip(jnp.exp(math.log(2.0) - 2.0794415 * jax.random.uniform(splits[3], (KERNELS,), jnp.float32) ** levels(splits[3], (KERNELS,), ((0, 2),), -0.2, 0.2)), 0.25, 2.0)
    target = draw_target(jax.random.fold_in(jax.random.fold_in(splits[5], part), 71), part)
    return dict(features=features, head_weight=head_weight, kernels=kernels, kernel_weights=kernel_weights, target=target)


precise = lax.Precision.HIGHEST
steepness = 2.0
threshold = 2.0

def band_tables(row_ids, band_len, full_len):
    frequency = jnp.arange(band_len, dtype=jnp.int32) - band_len // 2
    phases = jnp.mod(row_ids[:, None] * frequency[None, :], full_len)
    angles = phases.astype(jnp.float32) * (2.0 * math.pi / full_len)
    return (jnp.cos(angles), jnp.sin(angles))

def right_prod(lhs_part, lookup):
    return jnp.dot(lhs_part, lookup, precision=precise, preferred_element_type=jnp.float32)

def right_trans(lhs_part, lookup):
    return lax.dot_general(lhs_part, lookup, (((1,), (1,)), ((), ())), precision=precise, preferred_element_type=jnp.float32)

def batch_left(lookup, blocks):
    return jnp.einsum('rs,krt->kst', lookup, blocks, precision=precise, preferred_element_type=jnp.float32)

def batch_apply(lookup, blocks):
    return jnp.einsum('rs,kst->krt', lookup, blocks, precision=precise, preferred_element_type=jnp.float32)

def synthesize(filt_real, filt_imag, cos_rows, sin_rows, cos_full, sin_full):
    kern_count = filt_real.shape[0]
    band_len = filt_real.shape[-1]
    row_count = cos_rows.shape[0]
    q_real = (batch_apply(cos_rows, filt_real) - batch_apply(sin_rows, filt_imag)).reshape(kern_count * row_count, band_len)
    q_imag = (batch_apply(cos_rows, filt_imag) + batch_apply(sin_rows, filt_real)).reshape(kern_count * row_count, band_len)
    out_real = (right_trans(q_real, cos_full) - right_trans(q_imag, sin_full)) / band_len
    out_imag = (right_trans(q_real, sin_full) + right_trans(q_imag, cos_full)) / band_len
    return (out_real.reshape(kern_count, row_count, -1), out_imag.reshape(kern_count, row_count, -1))

def analyze(grad_real, grad_imag, cos_rows, sin_rows, cos_full, sin_full):
    kern_count, row_count, full_len = grad_real.shape
    band_len = cos_full.shape[1]
    flat_real = grad_real.reshape(kern_count * row_count, full_len)
    flat_imag = grad_imag.reshape(kern_count * row_count, full_len)
    b_real = (right_prod(flat_real, cos_full) + right_prod(flat_imag, sin_full)).reshape(kern_count, row_count, band_len)
    b_imag = (right_prod(flat_imag, cos_full) - right_prod(flat_real, sin_full)).reshape(kern_count, row_count, band_len)
    dy_real = (batch_left(cos_rows, b_real) + batch_left(sin_rows, b_imag)) / band_len
    dy_imag = (batch_left(cos_rows, b_imag) - batch_left(sin_rows, b_real)) / band_len
    return (dy_real, dy_imag)

def reference(features, head_weight, kernels, kernel_weights, target):
    cos_full, sin_full = band_tables(jnp.arange(N, dtype=jnp.int32), S, N)

    def add_channel(channel, running):
        return running + head_weight[channel] * features[channel].astype(jnp.float32)
    logits = lax.fori_loop(0, CHANNELS, add_channel, jnp.zeros((N, N), jnp.float32))
    mask_map = jax.nn.sigmoid(logits)
    half_real = right_prod(mask_map, cos_full)
    half_imag = -right_prod(mask_map, sin_full)
    spec_real = (batch_left(cos_full, half_real[None]) + batch_left(sin_full, half_imag[None]))[0] / N
    spec_imag = (batch_left(cos_full, half_imag[None]) - batch_left(sin_full, half_real[None]))[0] / N

    def field_of(kernel_id):
        gain = kernels[kernel_id]
        filt_real = gain[0] * spec_real - gain[1] * spec_imag
        filt_imag = gain[0] * spec_imag + gain[1] * spec_real
        return synthesize(filt_real[None], filt_imag[None], cos_full, sin_full, cos_full, sin_full)

    def add_power(running, kernel_id):
        field_real, field_imag = field_of(kernel_id)
        return (running + kernel_weights[kernel_id] * (field_real[0] ** 2 + field_imag[0] ** 2), None)
    intensity, _ = lax.scan(add_power, jnp.zeros((N, N), jnp.float32), jnp.arange(KERNELS, dtype=jnp.int32))
    resist = jax.nn.sigmoid(steepness * (intensity - threshold))
    grad_intensity = 2.0 * (resist - target.astype(jnp.float32)) * steepness * resist * (1.0 - resist)

    def add_grad(running, kernel_id):
        field_real, field_imag = field_of(kernel_id)
        factor = 2.0 * kernel_weights[kernel_id] * grad_intensity
        dy_real, dy_imag = analyze(factor[None] * field_real, factor[None] * field_imag, cos_full, sin_full, cos_full, sin_full)
        gain = kernels[kernel_id]
        dx_real = gain[0] * dy_real[0] + gain[1] * dy_imag[0]
        dx_imag = gain[0] * dy_imag[0] - gain[1] * dy_real[0]
        return ((running[0] + dx_real, running[1] + dx_imag), None)
    zero_band = jnp.zeros((S, S), jnp.float32)
    (grad_real, grad_imag), _ = lax.scan(add_grad, (zero_band, zero_band), jnp.arange(KERNELS, dtype=jnp.int32))
    q_real = right_prod(cos_full, grad_real) - right_prod(sin_full, grad_imag)
    q_imag = right_prod(cos_full, grad_imag) + right_prod(sin_full, grad_real)
    grad_mask = (right_trans(q_real, cos_full) - right_trans(q_imag, sin_full)) / N
    grad_logits = grad_mask * mask_map * (1.0 - mask_map)
    return (head_weight[:, None, None] * grad_logits[None]).astype(jnp.bfloat16)
```

```python
import functools
import math

import jax
import jax.numpy as jnp
import ml_dtypes
import numpy as np
from jax import lax
from jax.experimental import pallas as pl
from jax.experimental.pallas import tpu as pltpu
from jax.sharding import PartitionSpec as P

precise = lax.Precision.HIGHEST
steepness = 2.0
threshold = 2.0


def band_tables(row_ids, band_len, full_len):
    frequency = jnp.arange(band_len, dtype=jnp.int32) - band_len // 2
    phases = jnp.mod(row_ids[:, None] * frequency[None, :], full_len)
    angles = phases.astype(jnp.float32) * (2.0 * math.pi / full_len)
    return (jnp.cos(angles), jnp.sin(angles))


def right_prod(lhs_part, lookup):
    return jnp.dot(lhs_part, lookup, precision=precise, preferred_element_type=jnp.float32)


def right_trans(lhs_part, lookup):
    return lax.dot_general(
        lhs_part,
        lookup,
        (((1,), (1,)), ((), ())),
        precision=precise,
        preferred_element_type=jnp.float32,
    )


def batch_left(lookup, blocks):
    return jnp.einsum(
        "rs,krt->kst", lookup, blocks, precision=precise, preferred_element_type=jnp.float32
    )


def batch_apply(lookup, blocks):
    return jnp.einsum(
        "rs,kst->krt", lookup, blocks, precision=precise, preferred_element_type=jnp.float32
    )


def synthesize(filt_real, filt_imag, cos_rows, sin_rows, cos_full, sin_full):
    kern_count = filt_real.shape[0]
    band_len = filt_real.shape[-1]
    row_count = cos_rows.shape[0]
    q_real = (batch_apply(cos_rows, filt_real) - batch_apply(sin_rows, filt_imag)).reshape(
        kern_count * row_count, band_len
    )
    q_imag = (batch_apply(cos_rows, filt_imag) + batch_apply(sin_rows, filt_real)).reshape(
        kern_count * row_count, band_len
    )
    out_real = (right_trans(q_real, cos_full) - right_trans(q_imag, sin_full)) / band_len
    out_imag = (right_trans(q_real, sin_full) + right_trans(q_imag, cos_full)) / band_len
    return (
        out_real.reshape(kern_count, row_count, -1),
        out_imag.reshape(kern_count, row_count, -1),
    )


def analyze(grad_real, grad_imag, cos_rows, sin_rows, cos_full, sin_full):
    kern_count, row_count, full_len = grad_real.shape
    band_len = cos_full.shape[1]
    flat_real = grad_real.reshape(kern_count * row_count, full_len)
    flat_imag = grad_imag.reshape(kern_count * row_count, full_len)
    b_real = (right_prod(flat_real, cos_full) + right_prod(flat_imag, sin_full)).reshape(
        kern_count, row_count, band_len
    )
    b_imag = (right_prod(flat_imag, cos_full) - right_prod(flat_real, sin_full)).reshape(
        kern_count, row_count, band_len
    )
    dy_real = (batch_left(cos_rows, b_real) + batch_left(sin_rows, b_imag)) / band_len
    dy_imag = (batch_left(cos_rows, b_imag) - batch_left(sin_rows, b_real)) / band_len
    return (dy_real, dy_imag)


def conj_combine(kernels, dy_real, dy_imag):
    gain_real = kernels[:, 0]
    gain_imag = kernels[:, 1]
    dx_real = jnp.sum(gain_real * dy_real + gain_imag * dy_imag, axis=0)
    dx_imag = jnp.sum(gain_real * dy_imag - gain_imag * dy_real, axis=0)
    return (dx_real, dx_imag)


def band_part(mask_map, cos_rows, sin_rows, cos_full, sin_full):
    half_real = right_prod(mask_map, cos_full)
    half_imag = -right_prod(mask_map, sin_full)
    part_real = (batch_left(cos_rows, half_real[None]) + batch_left(sin_rows, half_imag[None]))[0]
    part_imag = (batch_left(cos_rows, half_imag[None]) - batch_left(sin_rows, half_real[None]))[0]
    return (part_real, part_imag)


def filter_all(kernels, spec_real, spec_imag):
    gain_real = kernels[:, 0]
    gain_imag = kernels[:, 1]
    filt_real = gain_real * spec_real[None] - gain_imag * spec_imag[None]
    filt_imag = gain_real * spec_imag[None] + gain_imag * spec_real[None]
    return (filt_real, filt_imag)


def resist_grad(intensity, target_rows):
    resist = jax.nn.sigmoid(steepness * (intensity - threshold))
    return 2.0 * (resist - target_rows.astype(jnp.float32)) * steepness * resist * (1.0 - resist)


def back_rows(grad_real, grad_imag, cos_rows, sin_rows, cos_full, sin_full, mask_map):
    full_len = cos_full.shape[0]
    q_real = right_prod(cos_rows, grad_real) - right_prod(sin_rows, grad_imag)
    q_imag = right_prod(cos_rows, grad_imag) + right_prod(sin_rows, grad_real)
    grad_mask = (right_trans(q_real, cos_full) - right_trans(q_imag, sin_full)) / full_len
    return grad_mask * mask_map * (1.0 - mask_map)


def on_device(features, head_weight, kernels, kernel_weights, target):
    row_count = target.shape[0]
    full_len = target.shape[1]
    band_len = kernels.shape[-1]
    cos_full, sin_full = band_tables(jnp.arange(full_len, dtype=jnp.int32), band_len, full_len)
    local_logits = jnp.sum(head_weight[:, None, None] * features.astype(jnp.float32), axis=0)
    row_ids = lax.axis_index("rows") * row_count + jnp.arange(row_count, dtype=jnp.int32)
    cos_rows, sin_rows = band_tables(row_ids, band_len, full_len)
    logits = lax.psum(local_logits, "kern")
    mask_map = jax.nn.sigmoid(logits)
    part_real, part_imag = band_part(mask_map, cos_rows, sin_rows, cos_full, sin_full)
    spec_real, spec_imag = lax.psum((part_real, part_imag), "rows")
    spec_real = spec_real / full_len
    spec_imag = spec_imag / full_len
    filt_real, filt_imag = filter_all(kernels, spec_real, spec_imag)
    field_real, field_imag = synthesize(
        filt_real, filt_imag, cos_rows, sin_rows, cos_full, sin_full
    )
    local_power = jnp.sum(
        kernel_weights[:, None, None] * (field_real * field_real + field_imag * field_imag), axis=0
    )
    intensity = lax.psum(local_power, "kern")
    grad_intensity = resist_grad(intensity, target)
    factor = 2.0 * kernel_weights[:, None, None] * grad_intensity[None]
    dy_real, dy_imag = analyze(
        factor * field_real, factor * field_imag, cos_rows, sin_rows, cos_full, sin_full
    )
    dy_real, dy_imag = lax.psum((dy_real, dy_imag), "rows")
    local_real, local_imag = conj_combine(kernels, dy_real, dy_imag)
    grad_real, grad_imag = lax.psum((local_real, local_imag), "kern")
    grad_logits = back_rows(grad_real, grad_imag, cos_rows, sin_rows, cos_full, sin_full, mask_map)
    return (head_weight[:, None, None] * grad_logits[None]).astype(jnp.bfloat16)


MESH = pl.DeviceIdType.MESH
f32 = jnp.float32
bf16 = jnp.bfloat16


def halves(table):
    high = table.astype(np.float32).astype(ml_dtypes.bfloat16)
    low = (table - high.astype(np.float64)).astype(np.float32).astype(ml_dtypes.bfloat16)
    return high, low


def make_tables(full_len, band_len, row_count, chips):
    frequency = np.arange(band_len) - band_len // 2
    phases = (np.arange(full_len)[:, None] * frequency[None, :]) % full_len
    angles = phases * (2.0 * math.pi / full_len)
    cos, sin = np.cos(angles), np.sin(angles)
    half = row_count // 2
    rf = np.block([[cos.T, sin.T], [-sin.T, cos.T]])
    rq = rf.reshape(2 * band_len, 2, chips, row_count).transpose(0, 2, 1, 3).reshape(rf.shape)
    by_core = lambda t: t.reshape(chips, 2, half, band_len)
    lt, lq, ld = [], [], []
    for core in range(2):
        c = by_core(cos)[:, core].reshape(-1, band_len)
        s = by_core(sin)[:, core].reshape(-1, band_len)
        lt.append(np.stack(halves(np.block([[c.T, s.T], [-s.T, c.T]]))))
    for chip in range(chips):
        for core in range(2):
            c, s = by_core(cos)[chip, core], by_core(sin)[chip, core]
            high, low = halves(np.block([[c, -s], [s, c]]))
            lq.append(np.concatenate([high, low], axis=0))
            ld.append(np.concatenate([high.T, low.T, high.T], axis=1))
    return (
        np.stack(halves(rf)),
        np.stack(halves(rf.T)),
        np.stack(halves(rq)),
        np.stack(lt),
        np.stack(lq),
        np.stack(ld),
    )


def split(x):
    high = x.astype(bf16)
    return high, (x - high.astype(f32)).astype(bf16)


def mm(a, b):
    return jnp.dot(a, b, preferred_element_type=f32)


def dot3(a, b_high, b_low):
    high, low = split(a)
    rows = a.shape[0]
    both = mm(jnp.concatenate([high, low], axis=0), b_high)
    return both[:rows] + both[rows:] + mm(high, b_low)


def fused(
    hw, kw, feat, tgt, ker_hbm, rf_hbm, rb_hbm, rq_hbm, lt_hbm, lq_hbm, ld_hbm,
    out,
    ker, rf, rb, rq, lt, lq, ld,
    logit_send, logit_recv, wts, hbuf, x_send, x_recv, gs, gbuf, ps, pbuf, pt, mask_buf,
    local_sem, pair_send, pair_recv, h_send_sem, h_recv_sem, g_send_sem, g_recv_sem, p_send_sem, p_recv_sem,
):
    chips, half, _ = hbuf.shape
    band = ker.shape[-1]
    full = feat.shape[-1]
    channels = feat.shape[0]
    kpc = ker.shape[1]
    kcount = 2 * kpc
    n = 2 * chips
    r = lax.axis_index("rows")
    c = lax.axis_index("kern")
    me = 2 * r + c
    partner = {"rows": r, "kern": 1 - c}

    def peer(d):
        p = lax.rem(me + d, n)
        return p, {"rows": p // 2, "kern": lax.rem(p, 2)}

    barrier = pltpu.get_barrier_semaphore()
    for d in range(1, n):
        pl.semaphore_signal(barrier, inc=1, device_id=peer(d)[1], device_id_type=MESH)

    def local(src, dst, i):
        copy = pltpu.make_async_copy(src, dst, local_sem.at[i])
        copy.start()
        return copy

    get_rb = local(rb_hbm, rb, 0)
    get_lt = local(lt_hbm.at[c], lt, 1)
    get_ker = local(ker_hbm, ker.at[c], 2)
    get_lq = local(lq_hbm.at[me], lq, 3)
    get_rf = local(rf_hbm, rf, 4)
    get_ld = local(ld_hbm.at[me], ld, 5)
    get_rq = local(rq_hbm, rq, 6)

    total = hw[0] * feat[0].astype(f32)
    for ch in range(1, channels):
        total = total + hw[ch] * feat[ch].astype(f32)
    logit_send[...] = total
    for k in range(kpc):
        wts[c, k : k + 1, :] = jnp.full((1, wts.shape[-1]), kw[k], f32)

    pl.semaphore_wait(barrier, n - 1)

    def remote(src, dst, send, recv, device):
        return pltpu.make_async_remote_copy(
            src_ref=src, dst_ref=dst, send_sem=send, recv_sem=recv, device_id=device, device_id_type=MESH
        )

    def pair(src, dst, i):
        return remote(src, dst, pair_send.at[i], pair_recv.at[i], partner)

    swap_logits = pair(logit_send, logit_recv, 0)
    swap_logits.start()
    swap_kernels = pair(ker_hbm, ker.at[c], 1)
    swap_weights = pair(wts.at[c], wts.at[c], 2)

    swap_logits.wait_recv()
    mask = jax.nn.sigmoid(logit_send[...] + logit_recv[...])
    mask_buf[...] = mask
    get_rb.wait()
    mine = mask_buf[pl.ds(pl.multiple_of(half * c, half), half), :]
    hbuf[r] = dot3(mine, rb[0, :full], rb[1, :full])
    sends = []
    for d in range(1, chips):
        p = lax.rem(r + d, chips)
        copy = remote(hbuf.at[r], hbuf.at[r], h_send_sem.at[d], h_recv_sem.at[r], {"rows": p, "kern": c})
        copy.start()
        sends.append(copy)
    swap_weights.start()
    swap_kernels.start()
    get_lt.wait()
    for d in range(1, chips):
        p = lax.rem(r + d, chips)
        remote(hbuf.at[p], hbuf.at[p], h_send_sem.at[d], h_recv_sem.at[p], {"rows": p, "kern": c}).wait_recv()
    rows = hbuf[...].reshape(chips * half, 2 * band)
    rh_high, rh_low = split(jnp.concatenate([rows[:, :band], rows[:, band:]], axis=0))
    x_send[...] = mm(lt[0], rh_high) + (mm(lt[1], rh_high) + mm(lt[0], rh_low))
    swap_x = pair(x_send, x_recv, 3)
    swap_x.start()
    get_ker.wait()
    get_lq.wait()
    pair(ker_hbm, ker.at[1 - c], 1).wait_recv()
    pair(wts.at[1 - c], wts.at[1 - c], 2).wait_recv()
    swap_x.wait_recv()
    x = (x_send[...] + x_recv[...]) * (1.0 / (full * band))
    xr, xi = x[:band], x[band:]

    kernel_of = lambda k, part: ker[k // kpc, k % kpc, part]
    weight_of = lambda k: wts[k // kpc, k % kpc : k % kpc + 1, :]
    qs = []
    for k0 in range(0, kcount, 2):
        columns = []
        for k in (k0, k0 + 1):
            kr, ki = kernel_of(k, 0), kernel_of(k, 1)
            columns.append(jnp.concatenate([kr * xr - ki * xi, kr * xi + ki * xr], axis=0))
        f_high, f_low = split(jnp.concatenate(columns, axis=1))
        both = mm(lq[...], f_high)
        q = both[: 2 * half] + both[2 * half :] + mm(lq[: 2 * half], f_low)
        for j in range(2):
            part = q[:, j * band : (j + 1) * band]
            qs.append(jnp.concatenate([part[:half], part[half:]], axis=1))
    get_rf.wait()
    field = dot3(jnp.concatenate(qs, axis=0), rf[0], rf[1])

    power = jnp.zeros((half, full), f32)
    for k in range(kcount):
        fr = field[k * half : (k + 1) * half, :full]
        fi = field[k * half : (k + 1) * half, full:]
        w = jnp.concatenate([weight_of(k)] * (full // wts.shape[-1]), axis=1)
        power = power + w * (fr * fr + fi * fi)
    target = tgt[pl.ds(pl.multiple_of(half * c, half), half), :].astype(f32)
    resist = jax.nn.sigmoid(steepness * (power - threshold))
    grad_power = 2.0 * (resist - target) * steepness * resist * (1.0 - resist)
    grads = []
    for k in range(kcount):
        w = jnp.concatenate([weight_of(k)] * (full // wts.shape[-1]), axis=1)
        factor = 2.0 * w * grad_power
        grads.append(jnp.concatenate([factor, factor], axis=1) * field[k * half : (k + 1) * half])
    b = dot3(jnp.concatenate(grads, axis=0), rb[0], rb[1])

    get_ld.wait()
    gr = jnp.zeros((band, band), f32)
    gi = jnp.zeros((band, band), f32)
    for k0 in range(0, kcount, 2):
        columns = []
        for k in (k0, k0 + 1):
            part = b[k * half : (k + 1) * half]
            columns.append(jnp.concatenate([part[:, :band], part[:, band:]], axis=0))
        b_high, b_low = split(jnp.concatenate(columns, axis=1))
        dy = mm(ld[...], jnp.concatenate([b_high, b_high, b_low], axis=0))
        for j, k in enumerate((k0, k0 + 1)):
            dr, di = dy[:band, j * band : (j + 1) * band], dy[band:, j * band : (j + 1) * band]
            kr, ki = kernel_of(k, 0), kernel_of(k, 1)
            gr = gr + (kr * dr + ki * di)
            gi = gi + (kr * di - ki * dr)
    gs[:, 0] = gr.T.reshape(n, band // n, band)
    gs[:, 1] = gi.T.reshape(n, band // n, band)

    for d in range(1, n):
        p, device = peer(d)
        copy = remote(gs.at[p], gbuf.at[d], g_send_sem.at[d], g_recv_sem.at[d], device)
        copy.start()
        sends.append(copy)
    get_rq.wait()
    mask = mask_buf[...]
    slope = mask * (1.0 - mask) * (1.0 / (full * band))
    g = gs[me]
    for d in range(1, n):
        remote(gs.at[0], gbuf.at[d], g_send_sem.at[d], g_recv_sem.at[d], peer(d)[1]).wait_recv()
        g = g + gbuf[d]
    q = dot3(jnp.concatenate([g[0], g[1]], axis=1), rq[0], rq[1])
    tiles = chips // 2
    for j in range(tiles):
        ps[j] = q[:, 128 * j : 128 * (j + 1)]
    pbuf[me] = ps[r // 2]
    for d in range(1, n):
        p, device = peer(d)
        copy = remote(ps.at[p // 4], pbuf.at[me], p_send_sem.at[d], p_recv_sem.at[me], device)
        copy.start()
        sends.append(copy)
    for d in range(1, n):
        p, device = peer(d)
        remote(ps.at[0], pbuf.at[p], p_send_sem.at[d], p_recv_sem.at[p], device).wait_recv()
    pt[...] = pbuf[...].reshape(band, 128).T
    base = pl.multiple_of(4 * half * lax.rem(r, 2), 4 * half)
    lhs = jnp.concatenate([pt[pl.ds(base, 2 * half), :], pt[pl.ds(base + 2 * half, 2 * half), :]], axis=1)
    grad_mask = dot3(lhs, rf[0, :, :full], rf[1, :, :full])
    out[...] = grad_mask * slope

    for copy in (swap_logits, swap_kernels, swap_weights, swap_x, *sends):
        copy.wait_send()


def fused_on_device(tables, chips, features, head_weight, kernels, kernel_weights, target):
    channels, row_count, full = features.shape
    kpc, _, band, _ = kernels.shape
    half = row_count // 2
    n = 2 * chips
    vmem = pl.BlockSpec(memory_space=pltpu.VMEM)
    smem = pl.BlockSpec(memory_space=pltpu.SMEM)
    anywhere = pl.BlockSpec(memory_space=pl.ANY)
    dma = pltpu.SemaphoreType.DMA
    rf, rb, rq, lt, lq, ld = tables
    grad_logits = pl.pallas_call(
        fused,
        out_shape=jax.ShapeDtypeStruct((row_count, full), f32),
        in_specs=[smem, smem, vmem, vmem] + [anywhere] * 7,
        out_specs=vmem,
        scratch_shapes=[
            pltpu.VMEM((2, kpc, 2, band, band), f32),
            pltpu.VMEM(rf.shape, bf16),
            pltpu.VMEM(rb.shape, bf16),
            pltpu.VMEM(rq.shape, bf16),
            pltpu.VMEM(lt.shape[1:], bf16),
            pltpu.VMEM(lq.shape[1:], bf16),
            pltpu.VMEM(ld.shape[1:], bf16),
            pltpu.VMEM((row_count, full), f32),
            pltpu.VMEM((row_count, full), f32),
            pltpu.VMEM((2, 8, 128), f32),
            pltpu.VMEM((chips, half, 2 * band), f32),
            pltpu.VMEM((2 * band, band), f32),
            pltpu.VMEM((2 * band, band), f32),
            pltpu.VMEM((n, 2, band // n, band), f32),
            pltpu.VMEM((n, 2, band // n, band), f32),
            pltpu.VMEM((chips // 2, band // n, 128), f32),
            pltpu.VMEM((n, band // n, 128), f32),
            pltpu.VMEM((128, band), f32),
            pltpu.VMEM((row_count, full), f32),
            dma((7,)),
            dma((4,)),
            dma((4,)),
            dma((chips,)),
            dma((chips,)),
            dma((n,)),
            dma((n,)),
            dma((n,)),
            dma((n,)),
        ],
        compiler_params=pltpu.CompilerParams(
            collective_id=0, has_side_effects=True, vmem_limit_bytes=32 * 1024 * 1024
        ),
    )(head_weight, kernel_weights, features, target, kernels, *[jnp.asarray(t) for t in (rf, rb, rq, lt, lq, ld)])
    return (head_weight[:, None, None] * grad_logits[None]).astype(jnp.bfloat16)


def choose(mesh, features, head_weight, kernels, kernel_weights, target):
    row_count, full = target.shape
    channels, kpc, band = features.shape[0], kernels.shape[0], kernels.shape[-1]
    chips = mesh.shape["rows"]
    fits = (
        mesh.shape["kern"] == 2 and row_count == 32 and chips == 8 and full == 256 and band == 128 and kpc == 4
    )
    if not fits:
        return on_device(features, head_weight, kernels, kernel_weights, target)
    tables = make_tables(full, band, row_count, chips)
    return fused_on_device(tables, chips, features, head_weight, kernels, kernel_weights, target)


def solution(mesh):
    return jax.shard_map(
        functools.partial(choose, mesh),
        mesh=mesh,
        in_specs=(
            P("kern", ("clips", "rows"), None),
            P("kern"),
            P("kern", None, None, None),
            P("kern"),
            P(("clips", "rows"), None),
        ),
        out_specs=P("kern", ("clips", "rows"), None),
        check_vma=False,
    )
```

```python
import functools
import math

import jax
import jax.numpy as jnp
import ml_dtypes
import numpy as np
from jax import lax
from jax.experimental import pallas as pl
from jax.experimental.pallas import tpu as pltpu
from jax.sharding import PartitionSpec as P

precise = lax.Precision.HIGHEST
steepness = 2.0
threshold = 2.0


def band_tables(row_ids, band_len, full_len):
    frequency = jnp.arange(band_len, dtype=jnp.int32) - band_len // 2
    phases = jnp.mod(row_ids[:, None] * frequency[None, :], full_len)
    angles = phases.astype(jnp.float32) * (2.0 * math.pi / full_len)
    return (jnp.cos(angles), jnp.sin(angles))


def right_prod(lhs_part, lookup):
    return jnp.dot(lhs_part, lookup, precision=precise, preferred_element_type=jnp.float32)


def right_trans(lhs_part, lookup):
    return lax.dot_general(
        lhs_part,
        lookup,
        (((1,), (1,)), ((), ())),
        precision=precise,
        preferred_element_type=jnp.float32,
    )


def batch_left(lookup, blocks):
    return jnp.einsum(
        "rs,krt->kst", lookup, blocks, precision=precise, preferred_element_type=jnp.float32
    )


def batch_apply(lookup, blocks):
    return jnp.einsum(
        "rs,kst->krt", lookup, blocks, precision=precise, preferred_element_type=jnp.float32
    )


def synthesize(filt_real, filt_imag, cos_rows, sin_rows, cos_full, sin_full):
    kern_count = filt_real.shape[0]
    band_len = filt_real.shape[-1]
    row_count = cos_rows.shape[0]
    q_real = (batch_apply(cos_rows, filt_real) - batch_apply(sin_rows, filt_imag)).reshape(
        kern_count * row_count, band_len
    )
    q_imag = (batch_apply(cos_rows, filt_imag) + batch_apply(sin_rows, filt_real)).reshape(
        kern_count * row_count, band_len
    )
    out_real = (right_trans(q_real, cos_full) - right_trans(q_imag, sin_full)) / band_len
    out_imag = (right_trans(q_real, sin_full) + right_trans(q_imag, cos_full)) / band_len
    return (
        out_real.reshape(kern_count, row_count, -1),
        out_imag.reshape(kern_count, row_count, -1),
    )


def analyze(grad_real, grad_imag, cos_rows, sin_rows, cos_full, sin_full):
    kern_count, row_count, full_len = grad_real.shape
    band_len = cos_full.shape[1]
    flat_real = grad_real.reshape(kern_count * row_count, full_len)
    flat_imag = grad_imag.reshape(kern_count * row_count, full_len)
    b_real = (right_prod(flat_real, cos_full) + right_prod(flat_imag, sin_full)).reshape(
        kern_count, row_count, band_len
    )
    b_imag = (right_prod(flat_imag, cos_full) - right_prod(flat_real, sin_full)).reshape(
        kern_count, row_count, band_len
    )
    dy_real = (batch_left(cos_rows, b_real) + batch_left(sin_rows, b_imag)) / band_len
    dy_imag = (batch_left(cos_rows, b_imag) - batch_left(sin_rows, b_real)) / band_len
    return (dy_real, dy_imag)


def conj_combine(kernels, dy_real, dy_imag):
    gain_real = kernels[:, 0]
    gain_imag = kernels[:, 1]
    dx_real = jnp.sum(gain_real * dy_real + gain_imag * dy_imag, axis=0)
    dx_imag = jnp.sum(gain_real * dy_imag - gain_imag * dy_real, axis=0)
    return (dx_real, dx_imag)


def band_part(mask_map, cos_rows, sin_rows, cos_full, sin_full):
    half_real = right_prod(mask_map, cos_full)
    half_imag = -right_prod(mask_map, sin_full)
    part_real = (batch_left(cos_rows, half_real[None]) + batch_left(sin_rows, half_imag[None]))[0]
    part_imag = (batch_left(cos_rows, half_imag[None]) - batch_left(sin_rows, half_real[None]))[0]
    return (part_real, part_imag)


def filter_all(kernels, spec_real, spec_imag):
    gain_real = kernels[:, 0]
    gain_imag = kernels[:, 1]
    filt_real = gain_real * spec_real[None] - gain_imag * spec_imag[None]
    filt_imag = gain_real * spec_imag[None] + gain_imag * spec_real[None]
    return (filt_real, filt_imag)


def resist_grad(intensity, target_rows):
    resist = jax.nn.sigmoid(steepness * (intensity - threshold))
    return 2.0 * (resist - target_rows.astype(jnp.float32)) * steepness * resist * (1.0 - resist)


def back_rows(grad_real, grad_imag, cos_rows, sin_rows, cos_full, sin_full, mask_map):
    full_len = cos_full.shape[0]
    q_real = right_prod(cos_rows, grad_real) - right_prod(sin_rows, grad_imag)
    q_imag = right_prod(cos_rows, grad_imag) + right_prod(sin_rows, grad_real)
    grad_mask = (right_trans(q_real, cos_full) - right_trans(q_imag, sin_full)) / full_len
    return grad_mask * mask_map * (1.0 - mask_map)


def on_device(features, head_weight, kernels, kernel_weights, target):
    row_count = target.shape[0]
    full_len = target.shape[1]
    band_len = kernels.shape[-1]
    cos_full, sin_full = band_tables(jnp.arange(full_len, dtype=jnp.int32), band_len, full_len)
    local_logits = jnp.sum(head_weight[:, None, None] * features.astype(jnp.float32), axis=0)
    row_ids = lax.axis_index("rows") * row_count + jnp.arange(row_count, dtype=jnp.int32)
    cos_rows, sin_rows = band_tables(row_ids, band_len, full_len)
    logits = lax.psum(local_logits, "kern")
    mask_map = jax.nn.sigmoid(logits)
    part_real, part_imag = band_part(mask_map, cos_rows, sin_rows, cos_full, sin_full)
    spec_real, spec_imag = lax.psum((part_real, part_imag), "rows")
    spec_real = spec_real / full_len
    spec_imag = spec_imag / full_len
    filt_real, filt_imag = filter_all(kernels, spec_real, spec_imag)
    field_real, field_imag = synthesize(
        filt_real, filt_imag, cos_rows, sin_rows, cos_full, sin_full
    )
    local_power = jnp.sum(
        kernel_weights[:, None, None] * (field_real * field_real + field_imag * field_imag), axis=0
    )
    intensity = lax.psum(local_power, "kern")
    grad_intensity = resist_grad(intensity, target)
    factor = 2.0 * kernel_weights[:, None, None] * grad_intensity[None]
    dy_real, dy_imag = analyze(
        factor * field_real, factor * field_imag, cos_rows, sin_rows, cos_full, sin_full
    )
    dy_real, dy_imag = lax.psum((dy_real, dy_imag), "rows")
    local_real, local_imag = conj_combine(kernels, dy_real, dy_imag)
    grad_real, grad_imag = lax.psum((local_real, local_imag), "kern")
    grad_logits = back_rows(grad_real, grad_imag, cos_rows, sin_rows, cos_full, sin_full, mask_map)
    return (head_weight[:, None, None] * grad_logits[None]).astype(jnp.bfloat16)


MESH = pl.DeviceIdType.MESH
VMEM_BYTES = 63 * 1024 * 1024
f32 = jnp.float32
bf16 = jnp.bfloat16


def halves(table):
    high = table.astype(np.float32).astype(ml_dtypes.bfloat16)
    low = (table - high.astype(np.float64)).astype(np.float32).astype(ml_dtypes.bfloat16)
    return high, low


def make_tables(full_len, band_len, row_count, chips):
    frequency = np.arange(band_len) - band_len // 2
    phases = (np.arange(full_len)[:, None] * frequency[None, :]) % full_len
    angles = phases * (2.0 * math.pi / full_len)
    cos, sin = np.cos(angles), np.sin(angles)
    half = row_count // 2
    rf = np.block([[cos.T, sin.T], [-sin.T, cos.T]])
    rq = rf.reshape(2 * band_len, 2, chips, row_count).transpose(0, 2, 1, 3).reshape(rf.shape)
    by_core = lambda t: t.reshape(chips, 2, half, band_len)
    lt, lq, ld, gt = [], [], [], []
    for core in range(2):
        c = by_core(cos)[:, core].reshape(-1, band_len)
        s = by_core(sin)[:, core].reshape(-1, band_len)
        mine = slice(core * band_len // 2, (core + 1) * band_len // 2)
        gt.append(np.stack(halves(np.concatenate([cos.T[mine], -sin.T[mine]], axis=0))))
        lt.append(np.stack(halves(np.block([[c.T, s.T], [-s.T, c.T]]))))
    for chip in range(chips):
        for core in range(2):
            c, s = by_core(cos)[chip, core], by_core(sin)[chip, core]
            high, low = halves(np.block([[c, -s], [s, c]]))
            lq.append(np.concatenate([high, low], axis=0))
            ld.append(np.concatenate([high.T, low.T, high.T], axis=1))
    return (
        np.stack(halves(rf)),
        np.stack(halves(rf.T)),
        np.stack(halves(rq)),
        np.stack(lt),
        np.stack(lq),
        np.stack(ld),
        np.stack(gt),
    )


def split(x):
    high = x.astype(bf16)
    return high, (x - high.astype(f32)).astype(bf16)


def mm(a, b):
    return jnp.dot(a, b, preferred_element_type=f32)


def dot3(a, b_high, b_low):
    high, low = split(a)
    rows = a.shape[0]
    both = mm(jnp.concatenate([high, low], axis=0), b_high)
    return both[:rows] + both[rows:] + mm(high, b_low)


def fused(
    hw_hbm, kw_hbm, feat_hbm, tgt_hbm, ker_hbm, rf_hbm, rb_hbm, rq_hbm, lt_hbm, lq_hbm, ld_hbm, gt_hbm,
    out,
    hw, kw, feat, tgt, ker, rf, rb, rq, lt, lq, ld, gt,
    logit_send, logit_recv, wts, hbuf, x_send, x_recv, gs, g_pair, g_sum, gbuf, ps, pbuf, pt, gm_send, gm_recv, mask_buf,
    local_sem, pair_send, pair_recv, h_send_sem, h_recv_sem, g_send_sem, g_recv_sem, p_send_sem, p_recv_sem,
):
    chips, half, _ = hbuf.shape
    band = ker.shape[-1]
    full = feat.shape[-1]
    channels = feat.shape[0]
    kpc = ker.shape[1]
    kcount = 2 * kpc
    n = 2 * chips
    r = lax.axis_index("rows")
    c = lax.axis_index("kern")
    me = 2 * r + c
    partner = {"rows": r, "kern": 1 - c}

    barrier = pltpu.get_barrier_semaphore()
    for d in range(1, chips):
        other = {"rows": lax.rem(r + d, chips), "kern": c}
        pl.semaphore_signal(barrier, inc=1, device_id=other, device_id_type=MESH)
    pl.semaphore_signal(barrier, inc=1, device_id=partner, device_id_type=MESH)

    pending = []

    def need(wait):
        wait()
        pending.remove(wait)

    def local(src, dst, i):
        copy = pltpu.make_async_copy(src, dst, local_sem.at[i])
        copy.start()
        pending.append(copy.wait)
        return pending[-1]

    get_hw = local(hw_hbm, hw, 7)
    get_feat = local(feat_hbm, feat, 8)
    get_kw = local(kw_hbm, kw, 9)
    get_tgt = local(tgt_hbm, tgt, 10)
    get_rb = local(rb_hbm, rb, 0)
    get_lt = local(lt_hbm.at[c], lt, 1)
    get_ker = local(ker_hbm, ker.at[c], 2)
    get_lq = local(lq_hbm.at[me], lq, 3)
    get_rf = local(rf_hbm, rf, 4)
    get_ld = local(ld_hbm.at[me], ld, 5)
    get_rq = local(rq_hbm, rq, 6)
    get_gt = local(gt_hbm.at[c], gt, 11)

    need(get_hw)
    need(get_feat)
    total = hw[0] * feat[0].astype(f32)
    for ch in range(1, channels):
        total = total + hw[ch] * feat[ch].astype(f32)
    logit_send[...] = total
    need(get_kw)
    for k in range(kpc):
        wts[c, k : k + 1, :] = jnp.full((1, wts.shape[-1]), kw[k], f32)

    pl.semaphore_wait(barrier, chips)

    def remote(src, dst, send, recv, device):
        return pltpu.make_async_remote_copy(
            src_ref=src, dst_ref=dst, send_sem=send, recv_sem=recv, device_id=device, device_id_type=MESH
        )

    def send(copy):
        copy.start()
        pending.append(copy.wait_send)

    def pair(src, dst, i):
        return remote(src, dst, pair_send.at[i], pair_recv.at[i], partner)

    swap_logits = pair(logit_send, logit_recv, 0)
    send(swap_logits)
    swap_kernels = pair(ker_hbm, ker.at[c], 1)
    swap_weights = pair(wts.at[c], wts.at[c], 2)

    swap_logits.wait_recv()
    mask = jax.nn.sigmoid(logit_send[...] + logit_recv[...])
    mask_buf[...] = mask
    need(get_rb)
    mine = mask_buf[pl.ds(pl.multiple_of(half * c, half), half), :]
    hbuf[r] = dot3(mine, rb[0, :full], rb[1, :full])
    for d in range(1, chips):
        p = lax.rem(r + d, chips)
        copy = remote(hbuf.at[r], hbuf.at[r], h_send_sem.at[d], h_recv_sem.at[r], {"rows": p, "kern": c})
        send(copy)
    send(swap_weights)
    send(swap_kernels)
    take_weights = pair(wts.at[1 - c], wts.at[1 - c], 2).wait_recv
    take_kernels = pair(ker_hbm, ker.at[1 - c], 1).wait_recv
    pending.extend((take_weights, take_kernels))
    need(get_lt)
    for d in range(1, chips):
        p = lax.rem(r + d, chips)
        remote(hbuf.at[p], hbuf.at[p], h_send_sem.at[d], h_recv_sem.at[p], {"rows": p, "kern": c}).wait_recv()
    rows = hbuf[...].reshape(chips * half, 2 * band)
    rh_high, rh_low = split(jnp.concatenate([rows[:, :band], rows[:, band:]], axis=0))
    x_send[...] = mm(lt[0], rh_high) + (mm(lt[1], rh_high) + mm(lt[0], rh_low))
    swap_x = pair(x_send, x_recv, 3)
    send(swap_x)
    need(get_ker)
    need(get_lq)
    need(take_kernels)
    need(take_weights)
    swap_x.wait_recv()
    x = (x_send[...] + x_recv[...]) * (1.0 / (full * band))
    xr, xi = x[:band], x[band:]

    kernel_of = lambda k, part: ker[k // kpc, k % kpc, part]
    weight_of = lambda k: wts[k // kpc, k % kpc : k % kpc + 1, :]
    qs = []
    for k0 in range(0, kcount, 2):
        columns = []
        for k in (k0, k0 + 1):
            kr, ki = kernel_of(k, 0), kernel_of(k, 1)
            columns.append(jnp.concatenate([kr * xr - ki * xi, kr * xi + ki * xr], axis=0))
        f_high, f_low = split(jnp.concatenate(columns, axis=1))
        both = mm(lq[...], f_high)
        q = both[: 2 * half] + both[2 * half :] + mm(lq[: 2 * half], f_low)
        for j in range(2):
            part = q[:, j * band : (j + 1) * band]
            qs.append(jnp.concatenate([part[:half], part[half:]], axis=1))
    need(get_rf)
    field = dot3(jnp.concatenate(qs, axis=0), rf[0], rf[1])

    power = jnp.zeros((half, full), f32)
    for k in range(kcount):
        fr = field[k * half : (k + 1) * half, :full]
        fi = field[k * half : (k + 1) * half, full:]
        w = jnp.concatenate([weight_of(k)] * (full // wts.shape[-1]), axis=1)
        power = power + w * (fr * fr + fi * fi)
    need(get_tgt)
    target = tgt[pl.ds(pl.multiple_of(half * c, half), half), :].astype(f32)
    resist = jax.nn.sigmoid(steepness * (power - threshold))
    grad_power = 2.0 * (resist - target) * steepness * resist * (1.0 - resist)
    grads = []
    for k in range(kcount):
        w = jnp.concatenate([weight_of(k)] * (full // wts.shape[-1]), axis=1)
        factor = 2.0 * w * grad_power
        grads.append(jnp.concatenate([factor, factor], axis=1) * field[k * half : (k + 1) * half])
    b = dot3(jnp.concatenate(grads, axis=0), rb[0], rb[1])

    need(get_ld)
    gr = jnp.zeros((band, band), f32)
    gi = jnp.zeros((band, band), f32)
    for k0 in range(0, kcount, 2):
        columns = []
        for k in (k0, k0 + 1):
            part = b[k * half : (k + 1) * half]
            columns.append(jnp.concatenate([part[:, :band], part[:, band:]], axis=0))
        b_high, b_low = split(jnp.concatenate(columns, axis=1))
        dy = mm(ld[...], jnp.concatenate([b_high, b_high, b_low], axis=0))
        for j, k in enumerate((k0, k0 + 1)):
            dr, di = dy[:band, j * band : (j + 1) * band], dy[band:, j * band : (j + 1) * band]
            kr, ki = kernel_of(k, 0), kernel_of(k, 1)
            gr = gr + (kr * dr + ki * di)
            gi = gi + (kr * di - ki * dr)
    gs[:, :, 0] = gr.T.reshape(2, chips, band // n, band)
    gs[:, :, 1] = gi.T.reshape(2, chips, band // n, band)
    swap_g = pair(gs.at[1 - c], g_pair, 4)
    send(swap_g)
    need(get_rq)
    need(get_gt)
    mask = mask_buf[...]
    slope = mask * (1.0 - mask) * (1.0 / (full * band))
    swap_g.wait_recv()
    g_sum[...] = gs[c] + g_pair[...]
    for d in range(1, chips):
        p = lax.rem(r + d, chips)
        send(remote(g_sum.at[p], gbuf.at[d], g_send_sem.at[d], g_recv_sem.at[d], {"rows": p, "kern": c}))
    g = g_sum[r]
    for d in range(1, chips):
        p = lax.rem(r + d, chips)
        remote(g_sum.at[p], gbuf.at[d], g_send_sem.at[d], g_recv_sem.at[d], {"rows": p, "kern": c}).wait_recv()
        g = g + gbuf[d]
    q = dot3(jnp.concatenate([g[0], g[1]], axis=1), rq[0], rq[1])
    for j in range(chips // 2):
        ps[j] = q[:, 128 * j : 128 * (j + 1)]
    pbuf[r] = ps[r // 2]
    for d in range(1, chips):
        p = lax.rem(r + d, chips)
        send(remote(ps.at[p // 2], pbuf.at[r], p_send_sem.at[d], p_recv_sem.at[r], {"rows": p, "kern": c}))
    for d in range(1, chips):
        p = lax.rem(r + d, chips)
        remote(ps.at[0], pbuf.at[p], p_send_sem.at[d], p_recv_sem.at[p], {"rows": p, "kern": c}).wait_recv()
    pt[...] = pbuf[...].reshape(band // 2, 128).T
    base = pl.multiple_of(4 * half * lax.rem(r, 2), 4 * half)
    lhs = jnp.concatenate([pt[pl.ds(base, 2 * half), :], pt[pl.ds(base + 2 * half, 2 * half), :]], axis=1)
    gm_send[...] = dot3(lhs, gt[0], gt[1])
    swap_gm = pair(gm_send, gm_recv, 5)
    send(swap_gm)
    swap_gm.wait_recv()
    out[...] = (gm_send[...] + gm_recv[...]) * slope
    for wait in list(pending):
        need(wait)


def fused_on_device(tables, chips, features, head_weight, kernels, kernel_weights, target):
    channels, row_count, full = features.shape
    kpc, _, band, _ = kernels.shape
    half = row_count // 2
    n = 2 * chips
    vmem = pl.BlockSpec(memory_space=pltpu.VMEM)
    hbm = pl.BlockSpec(memory_space=pltpu.HBM)
    dma = pltpu.SemaphoreType.DMA
    rf, rb, rq, lt, lq, ld, gt = tables
    grad_logits = pl.pallas_call(
        fused,
        out_shape=jax.ShapeDtypeStruct((row_count, full), f32),
        in_specs=[hbm] * 12,
        out_specs=vmem,
        scratch_shapes=[
            pltpu.SMEM(head_weight.shape, f32),
            pltpu.SMEM(kernel_weights.shape, f32),
            pltpu.VMEM(features.shape, bf16),
            pltpu.VMEM(target.shape, bf16),
            pltpu.VMEM((2, kpc, 2, band, band), f32),
            pltpu.VMEM(rf.shape, bf16),
            pltpu.VMEM(rb.shape, bf16),
            pltpu.VMEM(rq.shape, bf16),
            pltpu.VMEM(lt.shape[1:], bf16),
            pltpu.VMEM(lq.shape[1:], bf16),
            pltpu.VMEM(ld.shape[1:], bf16),
            pltpu.VMEM(gt.shape[1:], bf16),
            pltpu.VMEM((row_count, full), f32),
            pltpu.VMEM((row_count, full), f32),
            pltpu.VMEM((2, 8, 128), f32),
            pltpu.VMEM((chips, half, 2 * band), f32),
            pltpu.VMEM((2 * band, band), f32),
            pltpu.VMEM((2 * band, band), f32),
            pltpu.VMEM((2, chips, 2, band // n, band), f32),
            pltpu.VMEM((chips, 2, band // n, band), f32),
            pltpu.VMEM((chips, 2, band // n, band), f32),
            pltpu.VMEM((chips, 2, band // n, band), f32),
            pltpu.VMEM((chips // 2, band // n, 128), f32),
            pltpu.VMEM((chips, band // n, 128), f32),
            pltpu.VMEM((128, band // 2), f32),
            pltpu.VMEM((row_count, full), f32),
            pltpu.VMEM((row_count, full), f32),
            pltpu.VMEM((row_count, full), f32),
            dma((12,)),
            dma((6,)),
            dma((6,)),
            dma((chips,)),
            dma((chips,)),
            dma((chips,)),
            dma((chips,)),
            dma((chips,)),
            dma((chips,)),
        ],
        compiler_params=pltpu.CompilerParams(
            collective_id=0, has_side_effects=True, vmem_limit_bytes=VMEM_BYTES
        ),
    )(head_weight, kernel_weights, features, target, kernels, *[jnp.asarray(t) for t in tables])
    return (head_weight[:, None, None] * grad_logits[None]).astype(jnp.bfloat16)


def choose(mesh, features, head_weight, kernels, kernel_weights, target):
    row_count, full = target.shape
    channels, kpc, band = features.shape[0], kernels.shape[0], kernels.shape[-1]
    chips = mesh.shape["rows"]
    fits = (
        mesh.shape["kern"] == 2 and row_count == 32 and chips == 8 and full == 256 and band == 128 and kpc == 4
    )
    if not fits:
        return on_device(features, head_weight, kernels, kernel_weights, target)
    tables = make_tables(full, band, row_count, chips)
    return fused_on_device(tables, chips, features, head_weight, kernels, kernel_weights, target)


def solution(mesh):
    return jax.shard_map(
        functools.partial(choose, mesh),
        mesh=mesh,
        in_specs=(
            P("kern", ("clips", "rows"), None),
            P("kern"),
            P("kern", None, None, None),
            P("kern"),
            P(("clips", "rows"), None),
        ),
        out_specs=P("kern", ("clips", "rows"), None),
        check_vma=False,
    )
```

```python
import functools
import math

import jax
import jax.numpy as jnp
import ml_dtypes
import numpy as np
from jax import lax
from jax.experimental import pallas as pl
from jax.experimental.pallas import tpu as pltpu
from jax.sharding import PartitionSpec as P

precise = lax.Precision.HIGHEST
steepness = 2.0
threshold = 2.0


def band_tables(row_ids, band_len, full_len):
    frequency = jnp.arange(band_len, dtype=jnp.int32) - band_len // 2
    phases = jnp.mod(row_ids[:, None] * frequency[None, :], full_len)
    angles = phases.astype(jnp.float32) * (2.0 * math.pi / full_len)
    return (jnp.cos(angles), jnp.sin(angles))


def right_prod(lhs_part, lookup):
    return jnp.dot(lhs_part, lookup, precision=precise, preferred_element_type=jnp.float32)


def right_trans(lhs_part, lookup):
    return lax.dot_general(
        lhs_part,
        lookup,
        (((1,), (1,)), ((), ())),
        precision=precise,
        preferred_element_type=jnp.float32,
    )


def batch_left(lookup, blocks):
    return jnp.einsum(
        "rs,krt->kst", lookup, blocks, precision=precise, preferred_element_type=jnp.float32
    )


def batch_apply(lookup, blocks):
    return jnp.einsum(
        "rs,kst->krt", lookup, blocks, precision=precise, preferred_element_type=jnp.float32
    )


def synthesize(filt_real, filt_imag, cos_rows, sin_rows, cos_full, sin_full):
    kern_count = filt_real.shape[0]
    band_len = filt_real.shape[-1]
    row_count = cos_rows.shape[0]
    q_real = (batch_apply(cos_rows, filt_real) - batch_apply(sin_rows, filt_imag)).reshape(
        kern_count * row_count, band_len
    )
    q_imag = (batch_apply(cos_rows, filt_imag) + batch_apply(sin_rows, filt_real)).reshape(
        kern_count * row_count, band_len
    )
    out_real = (right_trans(q_real, cos_full) - right_trans(q_imag, sin_full)) / band_len
    out_imag = (right_trans(q_real, sin_full) + right_trans(q_imag, cos_full)) / band_len
    return (
        out_real.reshape(kern_count, row_count, -1),
        out_imag.reshape(kern_count, row_count, -1),
    )


def analyze(grad_real, grad_imag, cos_rows, sin_rows, cos_full, sin_full):
    kern_count, row_count, full_len = grad_real.shape
    band_len = cos_full.shape[1]
    flat_real = grad_real.reshape(kern_count * row_count, full_len)
    flat_imag = grad_imag.reshape(kern_count * row_count, full_len)
    b_real = (right_prod(flat_real, cos_full) + right_prod(flat_imag, sin_full)).reshape(
        kern_count, row_count, band_len
    )
    b_imag = (right_prod(flat_imag, cos_full) - right_prod(flat_real, sin_full)).reshape(
        kern_count, row_count, band_len
    )
    dy_real = (batch_left(cos_rows, b_real) + batch_left(sin_rows, b_imag)) / band_len
    dy_imag = (batch_left(cos_rows, b_imag) - batch_left(sin_rows, b_real)) / band_len
    return (dy_real, dy_imag)


def conj_combine(kernels, dy_real, dy_imag):
    gain_real = kernels[:, 0]
    gain_imag = kernels[:, 1]
    dx_real = jnp.sum(gain_real * dy_real + gain_imag * dy_imag, axis=0)
    dx_imag = jnp.sum(gain_real * dy_imag - gain_imag * dy_real, axis=0)
    return (dx_real, dx_imag)


def band_part(mask_map, cos_rows, sin_rows, cos_full, sin_full):
    half_real = right_prod(mask_map, cos_full)
    half_imag = -right_prod(mask_map, sin_full)
    part_real = (batch_left(cos_rows, half_real[None]) + batch_left(sin_rows, half_imag[None]))[0]
    part_imag = (batch_left(cos_rows, half_imag[None]) - batch_left(sin_rows, half_real[None]))[0]
    return (part_real, part_imag)


def filter_all(kernels, spec_real, spec_imag):
    gain_real = kernels[:, 0]
    gain_imag = kernels[:, 1]
    filt_real = gain_real * spec_real[None] - gain_imag * spec_imag[None]
    filt_imag = gain_real * spec_imag[None] + gain_imag * spec_real[None]
    return (filt_real, filt_imag)


def resist_grad(intensity, target_rows):
    resist = jax.nn.sigmoid(steepness * (intensity - threshold))
    return 2.0 * (resist - target_rows.astype(jnp.float32)) * steepness * resist * (1.0 - resist)


def back_rows(grad_real, grad_imag, cos_rows, sin_rows, cos_full, sin_full, mask_map):
    full_len = cos_full.shape[0]
    q_real = right_prod(cos_rows, grad_real) - right_prod(sin_rows, grad_imag)
    q_imag = right_prod(cos_rows, grad_imag) + right_prod(sin_rows, grad_real)
    grad_mask = (right_trans(q_real, cos_full) - right_trans(q_imag, sin_full)) / full_len
    return grad_mask * mask_map * (1.0 - mask_map)


def on_device(features, head_weight, kernels, kernel_weights, target):
    row_count = target.shape[0]
    full_len = target.shape[1]
    band_len = kernels.shape[-1]
    cos_full, sin_full = band_tables(jnp.arange(full_len, dtype=jnp.int32), band_len, full_len)
    local_logits = jnp.sum(head_weight[:, None, None] * features.astype(jnp.float32), axis=0)
    row_ids = lax.axis_index("rows") * row_count + jnp.arange(row_count, dtype=jnp.int32)
    cos_rows, sin_rows = band_tables(row_ids, band_len, full_len)
    logits = lax.psum(local_logits, "kern")
    mask_map = jax.nn.sigmoid(logits)
    part_real, part_imag = band_part(mask_map, cos_rows, sin_rows, cos_full, sin_full)
    spec_real, spec_imag = lax.psum((part_real, part_imag), "rows")
    spec_real = spec_real / full_len
    spec_imag = spec_imag / full_len
    filt_real, filt_imag = filter_all(kernels, spec_real, spec_imag)
    field_real, field_imag = synthesize(
        filt_real, filt_imag, cos_rows, sin_rows, cos_full, sin_full
    )
    local_power = jnp.sum(
        kernel_weights[:, None, None] * (field_real * field_real + field_imag * field_imag), axis=0
    )
    intensity = lax.psum(local_power, "kern")
    grad_intensity = resist_grad(intensity, target)
    factor = 2.0 * kernel_weights[:, None, None] * grad_intensity[None]
    dy_real, dy_imag = analyze(
        factor * field_real, factor * field_imag, cos_rows, sin_rows, cos_full, sin_full
    )
    dy_real, dy_imag = lax.psum((dy_real, dy_imag), "rows")
    local_real, local_imag = conj_combine(kernels, dy_real, dy_imag)
    grad_real, grad_imag = lax.psum((local_real, local_imag), "kern")
    grad_logits = back_rows(grad_real, grad_imag, cos_rows, sin_rows, cos_full, sin_full, mask_map)
    return (head_weight[:, None, None] * grad_logits[None]).astype(jnp.bfloat16)


MESH = pl.DeviceIdType.MESH
VMEM_BYTES = 63 * 1024 * 1024
f32 = jnp.float32
bf16 = jnp.bfloat16


def halves(table):
    high = table.astype(np.float32).astype(ml_dtypes.bfloat16)
    low = (table - high.astype(np.float64)).astype(np.float32).astype(ml_dtypes.bfloat16)
    return high, low


def make_tables(full_len, band_len, row_count, chips):
    frequency = np.arange(band_len) - band_len // 2
    phases = (np.arange(full_len)[:, None] * frequency[None, :]) % full_len
    angles = phases * (2.0 * math.pi / full_len)
    cos, sin = np.cos(angles), np.sin(angles)
    half = row_count // 2
    rf = np.block([[cos.T, sin.T], [-sin.T, cos.T]])
    qt = rf.T.reshape(2, chips, 2, half, 2 * band_len).transpose(0, 2, 1, 3, 4).reshape(2 * full_len, 2 * band_len)
    by_core = lambda t: t.reshape(chips, 2, half, band_len)
    lt, lq, ld = [], [], []
    for core in range(2):
        c = by_core(cos)[:, core].reshape(-1, band_len)
        s = by_core(sin)[:, core].reshape(-1, band_len)
        lt.append(np.stack(halves(np.block([[c.T, s.T], [-s.T, c.T]]))))
    for chip in range(chips):
        for core in range(2):
            c, s = by_core(cos)[chip, core], by_core(sin)[chip, core]
            high, low = halves(np.block([[c, -s], [s, c]]))
            lq.append(np.concatenate([high, low], axis=0))
            ld.append(np.concatenate([high.T, low.T, high.T], axis=1))
    return (
        np.stack(halves(rf)),
        np.stack(halves(rf.T)),
        np.stack(halves(qt)),
        np.stack(lt),
        np.stack(lq),
        np.stack(ld),
    )


def split(x):
    high = x.astype(bf16)
    return high, (x - high.astype(f32)).astype(bf16)


def mm(a, b):
    return jnp.dot(a, b, preferred_element_type=f32)


def dot3(a, b_high, b_low):
    high, low = split(a)
    rows = a.shape[0]
    both = mm(jnp.concatenate([high, low], axis=0), b_high)
    return both[:rows] + both[rows:] + mm(high, b_low)


def fused(
    hw_hbm, kw_hbm, feat_hbm, tgt_hbm, ker_hbm, rf_hbm, rb_hbm, qt_hbm, lt_hbm, lq_hbm, ld_hbm,
    out,
    hw, kw, feat, tgt, ker, rf, rb, qt, lt, lq, ld,
    logit_send, logit_recv, wts, hbuf, x_send, x_recv, qbuf, gs, g_pair, g_sum, gbuf, final, mask_buf,
    local_sem, pair_send, pair_recv, h_send_sem, h_recv_sem, g_send_sem, g_recv_sem,
):
    chips, half, _ = hbuf.shape
    band = ker.shape[-1]
    full = feat.shape[-1]
    channels = feat.shape[0]
    kpc = ker.shape[1]
    kcount = 2 * kpc
    r = lax.axis_index("rows")
    c = lax.axis_index("kern")
    me = 2 * r + c
    partner = {"rows": r, "kern": 1 - c}

    barrier = pltpu.get_barrier_semaphore()
    for d in range(1, chips):
        other = {"rows": lax.rem(r + d, chips), "kern": c}
        pl.semaphore_signal(barrier, inc=1, device_id=other, device_id_type=MESH)
    pl.semaphore_signal(barrier, inc=1, device_id=partner, device_id_type=MESH)

    pending = []

    def need(wait):
        wait()
        pending.remove(wait)

    def local(src, dst, i):
        copy = pltpu.make_async_copy(src, dst, local_sem.at[i])
        copy.start()
        pending.append(copy.wait)
        return pending[-1]

    get_hw = local(hw_hbm, hw, 7)
    get_feat = local(feat_hbm, feat, 8)
    get_kw = local(kw_hbm, kw, 9)
    get_tgt = local(tgt_hbm, tgt, 10)
    get_rb = local(rb_hbm, rb, 0)
    get_lt = local(lt_hbm.at[c], lt, 1)
    get_ker = local(ker_hbm, ker.at[c], 2)
    get_lq = local(lq_hbm.at[me], lq, 3)
    get_rf = local(rf_hbm, rf, 4)
    get_ld = local(ld_hbm.at[me], ld, 5)
    get_qt = local(qt_hbm, qt, 6)

    need(get_hw)
    need(get_feat)
    total = hw[0] * feat[0].astype(f32)
    for ch in range(1, channels):
        total = total + hw[ch] * feat[ch].astype(f32)
    logit_send[...] = total
    need(get_kw)
    for k in range(kpc):
        wts[c, k : k + 1, :] = jnp.full((1, wts.shape[-1]), kw[k], f32)

    pl.semaphore_wait(barrier, chips)

    def remote(src, dst, send, recv, device):
        return pltpu.make_async_remote_copy(
            src_ref=src, dst_ref=dst, send_sem=send, recv_sem=recv, device_id=device, device_id_type=MESH
        )

    def send(copy):
        copy.start()
        pending.append(copy.wait_send)

    def pair(src, dst, i):
        return remote(src, dst, pair_send.at[i], pair_recv.at[i], partner)

    swap_logits = pair(logit_send, logit_recv, 0)
    send(swap_logits)
    swap_kernels = pair(ker_hbm, ker.at[c], 1)
    swap_weights = pair(wts.at[c], wts.at[c], 2)

    swap_logits.wait_recv()
    mask = jax.nn.sigmoid(logit_send[...] + logit_recv[...])
    mask_buf[...] = mask
    need(get_rb)
    mine = mask_buf[pl.ds(pl.multiple_of(half * c, half), half), :]
    hbuf[r] = dot3(mine, rb[0, :full], rb[1, :full])
    for d in range(1, chips):
        p = lax.rem(r + d, chips)
        copy = remote(hbuf.at[r], hbuf.at[r], h_send_sem.at[d], h_recv_sem.at[r], {"rows": p, "kern": c})
        send(copy)
    send(swap_weights)
    send(swap_kernels)
    take_weights = pair(wts.at[1 - c], wts.at[1 - c], 2).wait_recv
    take_kernels = pair(ker_hbm, ker.at[1 - c], 1).wait_recv
    pending.extend((take_weights, take_kernels))
    need(get_lt)
    for d in range(1, chips):
        p = lax.rem(r + d, chips)
        remote(hbuf.at[p], hbuf.at[p], h_send_sem.at[d], h_recv_sem.at[p], {"rows": p, "kern": c}).wait_recv()
    rows = hbuf[...].reshape(chips * half, 2 * band)
    rh_high, rh_low = split(jnp.concatenate([rows[:, :band], rows[:, band:]], axis=0))
    x_send[...] = mm(lt[0], rh_high) + (mm(lt[1], rh_high) + mm(lt[0], rh_low))
    swap_x = pair(x_send, x_recv, 3)
    send(swap_x)
    need(get_ker)
    need(get_lq)
    need(take_kernels)
    need(take_weights)
    swap_x.wait_recv()
    x = (x_send[...] + x_recv[...]) * (1.0 / (full * band))
    xr, xi = x[:band], x[band:]

    kernel_of = lambda k, part: ker[k // kpc, k % kpc, part]
    weight_of = lambda k: wts[k // kpc, k % kpc : k % kpc + 1, :]
    qs = []
    for k0 in range(0, kcount, 2):
        columns = []
        for k in (k0, k0 + 1):
            kr, ki = kernel_of(k, 0), kernel_of(k, 1)
            columns.append(jnp.concatenate([kr * xr - ki * xi, kr * xi + ki * xr], axis=0))
        f_high, f_low = split(jnp.concatenate(columns, axis=1))
        both = mm(lq[...], f_high)
        q = both[: 2 * half] + both[2 * half :] + mm(lq[: 2 * half], f_low)
        for j in range(2):
            part = q[:, j * band : (j + 1) * band]
            qs.append(jnp.concatenate([part[:half], part[half:]], axis=1))
    need(get_rf)
    field = dot3(jnp.concatenate(qs, axis=0), rf[0], rf[1])

    power = jnp.zeros((half, full), f32)
    for k in range(kcount):
        fr = field[k * half : (k + 1) * half, :full]
        fi = field[k * half : (k + 1) * half, full:]
        w = jnp.concatenate([weight_of(k)] * (full // wts.shape[-1]), axis=1)
        power = power + w * (fr * fr + fi * fi)
    need(get_tgt)
    target = tgt[pl.ds(pl.multiple_of(half * c, half), half), :].astype(f32)
    resist = jax.nn.sigmoid(steepness * (power - threshold))
    grad_power = 2.0 * (resist - target) * steepness * resist * (1.0 - resist)
    grads = []
    for k in range(kcount):
        w = jnp.concatenate([weight_of(k)] * (full // wts.shape[-1]), axis=1)
        factor = 2.0 * w * grad_power
        grads.append(jnp.concatenate([factor, factor], axis=1) * field[k * half : (k + 1) * half])
    b = dot3(jnp.concatenate(grads, axis=0), rb[0], rb[1])

    need(get_ld)
    gr = jnp.zeros((band, band), f32)
    gi = jnp.zeros((band, band), f32)
    for k0 in range(0, kcount, 2):
        columns = []
        for k in (k0, k0 + 1):
            part = b[k * half : (k + 1) * half]
            columns.append(jnp.concatenate([part[:, :band], part[:, band:]], axis=0))
        b_high, b_low = split(jnp.concatenate(columns, axis=1))
        dy = mm(ld[...], jnp.concatenate([b_high, b_high, b_low], axis=0))
        for j, k in enumerate((k0, k0 + 1)):
            dr, di = dy[:band, j * band : (j + 1) * band], dy[band:, j * band : (j + 1) * band]
            kr, ki = kernel_of(k, 0), kernel_of(k, 1)
            gr = gr + (kr * dr + ki * di)
            gi = gi + (kr * di - ki * dr)
    need(get_qt)
    g_high, g_low = split(jnp.concatenate([gr, gi], axis=0))
    q = mm(qt[0], g_high) + (mm(qt[1], g_high) + mm(qt[0], g_low))
    qbuf[...] = jnp.concatenate([q[:full], q[full:]], axis=1).reshape(qbuf.shape)

    def back(core):
        return dot3(qbuf[core], rf[0, :, :full], rf[1, :, :full]).reshape(chips, half, full)

    gs[...] = back(1 - c)
    swap_g = pair(gs, g_pair, 4)
    send(swap_g)
    g_sum[...] = back(c)
    mask = mask_buf[pl.ds(pl.multiple_of(half * c, half), half), :]
    slope = mask * (1.0 - mask) * (1.0 / (full * band))
    swap_g.wait_recv()
    g_sum[...] = g_sum[...] + g_pair[...]
    for d in range(1, chips):
        p = lax.rem(r + d, chips)
        send(remote(g_sum.at[p], gbuf.at[d], g_send_sem.at[d], g_recv_sem.at[d], {"rows": p, "kern": c}))
    g = g_sum[r]
    for d in range(1, chips):
        p = lax.rem(r + d, chips)
        remote(g_sum.at[p], gbuf.at[d], g_send_sem.at[d], g_recv_sem.at[d], {"rows": p, "kern": c}).wait_recv()
        g = g + gbuf[d]
    final[c] = g * slope
    send(pair(final.at[c], final.at[c], 5))
    pair(final.at[1 - c], final.at[1 - c], 5).wait_recv()
    out[...] = final[...].reshape(out.shape)
    for wait in list(pending):
        need(wait)


def fused_on_device(tables, chips, features, head_weight, kernels, kernel_weights, target):
    channels, row_count, full = features.shape
    kpc, _, band, _ = kernels.shape
    half = row_count // 2
    vmem = pl.BlockSpec(memory_space=pltpu.VMEM)
    hbm = pl.BlockSpec(memory_space=pltpu.HBM)
    dma = pltpu.SemaphoreType.DMA
    rf, rb, qt, lt, lq, ld = tables
    grad_logits = pl.pallas_call(
        fused,
        out_shape=jax.ShapeDtypeStruct((row_count, full), f32),
        in_specs=[hbm] * 11,
        out_specs=vmem,
        scratch_shapes=[
            pltpu.SMEM(head_weight.shape, f32),
            pltpu.SMEM(kernel_weights.shape, f32),
            pltpu.VMEM(features.shape, bf16),
            pltpu.VMEM(target.shape, bf16),
            pltpu.VMEM((2, kpc, 2, band, band), f32),
            pltpu.VMEM(rf.shape, bf16),
            pltpu.VMEM(rb.shape, bf16),
            pltpu.VMEM(qt.shape, bf16),
            pltpu.VMEM(lt.shape[1:], bf16),
            pltpu.VMEM(lq.shape[1:], bf16),
            pltpu.VMEM(ld.shape[1:], bf16),
            pltpu.VMEM((row_count, full), f32),
            pltpu.VMEM((row_count, full), f32),
            pltpu.VMEM((2, 8, 128), f32),
            pltpu.VMEM((chips, half, 2 * band), f32),
            pltpu.VMEM((2 * band, band), f32),
            pltpu.VMEM((2 * band, band), f32),
            pltpu.VMEM((2, chips * half, 2 * band), f32),
            pltpu.VMEM((chips, half, full), f32),
            pltpu.VMEM((chips, half, full), f32),
            pltpu.VMEM((chips, half, full), f32),
            pltpu.VMEM((chips, half, full), f32),
            pltpu.VMEM((2, half, full), f32),
            pltpu.VMEM((row_count, full), f32),
            dma((11,)),
            dma((6,)),
            dma((6,)),
            dma((chips,)),
            dma((chips,)),
            dma((chips,)),
            dma((chips,)),
        ],
        compiler_params=pltpu.CompilerParams(
            collective_id=0, has_side_effects=True, vmem_limit_bytes=VMEM_BYTES
        ),
    )(head_weight, kernel_weights, features, target, kernels, *[jnp.asarray(t) for t in tables])
    return (head_weight[:, None, None] * grad_logits[None]).astype(jnp.bfloat16)


def choose(mesh, features, head_weight, kernels, kernel_weights, target):
    row_count, full = target.shape
    channels, kpc, band = features.shape[0], kernels.shape[0], kernels.shape[-1]
    chips = mesh.shape["rows"]
    fits = (
        mesh.shape["kern"] == 2 and row_count == 32 and chips == 8 and full == 256 and band == 128 and kpc == 4
    )
    if not fits:
        return on_device(features, head_weight, kernels, kernel_weights, target)
    tables = make_tables(full, band, row_count, chips)
    return fused_on_device(tables, chips, features, head_weight, kernels, kernel_weights, target)


def solution(mesh):
    return jax.shard_map(
        functools.partial(choose, mesh),
        mesh=mesh,
        in_specs=(
            P("kern", ("clips", "rows"), None),
            P("kern"),
            P("kern", None, None, None),
            P("kern"),
            P(("clips", "rows"), None),
        ),
        out_specs=P("kern", ("clips", "rows"), None),
        check_vma=False,
    )
```
